512 devices in a mesh: gx: 16 (over z), gy: 4 (over x), gz: 8 (over y, core).
Axes of the slice: x: 4, y: 4, z: 16, core: 2. Of those that a mesh axis runs over, the one named last changes fastest.
Arguments:
- voxels: bfloat16 [128, 32, 32, 256], P('gx', 'gy', 'gz'), may hold values from -6 to 6
- conv_first: bfloat16 [27, 256, 256], P(None, None, 'gx'), may hold values from -0.078125 to 0.078125
- conv_second: bfloat16 [27, 256, 256], P(None, None, 'gx'), may hold values from -0.078125 to 0.078125
- head_weight: bfloat16 [256, 768], replicated, may hold values from -0.375 to 0.375
- teacher_in: bfloat16 [512, 768], P(None, 'gx'), may hold values from -0.25 to 0.25
- teacher_out: bfloat16 [768, 768], P(None, 'gx'), may hold values from -0.21875 to 0.21875
- tile_feats: bfloat16 [64, 256, 512], P('gx'), may hold values from -6 to 6
- interpolation: bfloat16 [8, 8, 8, 8, 256], replicated, may hold values from -0.125 to 0.125
- tile_lists: int32 [16, 4, 8, 8], P(None, 'gy', 'gz'), may hold values from 0 to 63, as said below
Outputs:
- prediction: bfloat16 [128, 32, 32, 768], P('gx', 'gy', 'gz')
- hidden_grad: bfloat16 [128, 32, 32, 256], P('gx', 'gy', 'gz')
The draws below stay inside these ranges and needn't reach their ends.
Inputs may be any that keep to these rules, and one draw needn't show every extreme that they name: `tile_lists`: the 8 tiles of one brick lie in 8 different camera shards (tile t in shard t // 4); the two devices of one brick along gz (indices 2m and 2m+1) carry the same list.
All inputs are finite; a program needn't handle non-finite values.
Results may differ from the reference program's by a relative error of at most 0.0075.
Values may be sent and summed in bfloat16 or wider, within the bound.
A program may use at most 128 MiB of HBM per device.

```python
import jax
import jax.numpy as jnp
from jax import lax

CH = 256
DT = 768
CR = 512
PIX = 256
BRICK = 8
TILE_DEV = 4
SLOTS = 8
VX = 128
VY = 32
VZ = 32
TILES = 64
N_GX = 16
N_GY = 4
N_GZ = 8


def draw_tile_lists(key, part):
    key = jax.random.fold_in(key, 11)
    key_start, key_offset, key_local = jax.random.split(key, 3)
    bricks = N_GX * N_GY * (N_GZ // 2)
    starts = jax.random.randint(key_start, (bricks,), 0, N_GX)
    offsets = jax.vmap(lambda single: jax.random.permutation(single, N_GX - 1)[:SLOTS - 1] + 1)(jax.random.split(key_offset, bricks))
    offsets = jnp.concatenate([jnp.zeros((bricks, 1), jnp.int32), offsets.astype(jnp.int32)], axis=1)
    leading = (jnp.arange(bricks) == 0)[:, None]
    starts = jnp.where(leading[:, 0], N_GX - 1, starts)
    offsets = jnp.where(leading, jnp.arange(SLOTS)[None, :], offsets)
    owners = (starts[:, None] + offsets) % N_GX
    local_ids = jax.random.randint(key_local, (bricks, SLOTS), 0, TILE_DEV)
    local_ids = jnp.where(leading, jnp.where(jnp.arange(SLOTS)[None, :] == 0, TILE_DEV - 1, 0), local_ids)
    brick_lists = (owners * TILE_DEV + local_ids).reshape(N_GX, N_GY, N_GZ // 2, SLOTS)
    return jnp.repeat(brick_lists, 2, axis=2).astype(jnp.int32)


def block_scale(rng, shape, shards, smallest, largest):
    factor_of, own = 1.0, jax.random.fold_in(rng, 6)
    for dim, parts in shards:
        heights = jnp.exp(jax.random.uniform(jax.random.fold_in(own, dim), (parts,), jnp.float32, smallest / len(shards), largest / len(shards)))
        factor_of = factor_of * jnp.repeat(heights, shape[dim] // parts).reshape([-1 if axis == dim else 1 for axis in range(len(shape))])
    return factor_of


def gaussian(stream_key, dims, width, bound, shards=(), kind=jnp.bfloat16):
    array = jax.random.normal(stream_key, dims, jnp.float32) * width
    if len(shards) > 0:
        array = block_scale(stream_key, dims, shards, -0.22, 0.18) * array
    return jnp.clip(array, min=-bound, max=bound).astype(kind)


def setup_inputs(seed: int = 0) -> dict:
    streams_of = jax.random.split(jax.random.key(seed), 10)
    return {
        "voxels": gaussian(streams_of[0], (VX, VY, VZ, CH), 1.0, 6.0, ((0, 16), (1, 4), (2, 8))),
        "conv_first": gaussian(streams_of[1], (27, CH, CH), (27 * CH) ** -0.5, 0.078125, ((2, 16),)),
        "conv_second": gaussian(streams_of[2], (27, CH, CH), (27 * CH) ** -0.5, 0.078125, ((2, 16),)),
        "head_weight": gaussian(streams_of[3], (CH, DT), CH ** -0.5, 0.375),
        "teacher_in": gaussian(streams_of[4], (CR, DT), CR ** -0.5, 0.25, ((1, 16),)),
        "teacher_out": gaussian(streams_of[5], (DT, DT), DT ** -0.5, 0.21875, ((1, 16),)),
        "tile_feats": gaussian(streams_of[6], (TILES, PIX, CR), 1.0, 6.0, ((0, 16),)),
        "interpolation": gaussian(streams_of[7], (SLOTS, BRICK, BRICK, BRICK, PIX), (SLOTS * PIX) ** -0.5, 0.125),
        "tile_lists": draw_tile_lists(jax.random.fold_in(streams_of[9], 71), 0),
    }


offset_table = [(along_x, along_y, along_z) for along_x in range(3) for along_y in range(3) for along_z in range(3)]

def gather_patches(padded, count_x, count_y, count_z, flipped):
    pieces = []
    for along_x, along_y, along_z in offset_table:
        if flipped:
            corner = (2 - along_x, 2 - along_y, 2 - along_z, 0)
        else:
            corner = (along_x, along_y, along_z, 0)
        finish = (corner[0] + count_x, corner[1] + count_y, corner[2] + count_z, padded.shape[3])
        pieces.append(lax.slice(padded, corner, finish))
    return jnp.concatenate(pieces, axis=-1).reshape(count_x * count_y * count_z, -1)

def convolve(field, matrix, flipped):
    padded = jnp.pad(field, ((1, 1), (1, 1), (1, 1), (0, 0)))
    depth_y = field.shape[1]
    depth_z = field.shape[2]

    def one_slab(position):
        window = lax.dynamic_slice_in_dim(padded, position, 3, 0)
        patches = gather_patches(window, 1, depth_y, depth_z, flipped)
        return jnp.dot(patches, matrix, preferred_element_type=jnp.float32).reshape(depth_y, depth_z, -1)
    return lax.map(one_slab, jnp.arange(field.shape[0], dtype=jnp.int32))

def teacher_features(source, first_weight, second_weight):
    count_tiles, pixels, channels = source.shape
    hidden_units = jax.nn.silu(jnp.dot(source.reshape(-1, channels), first_weight, preferred_element_type=jnp.float32)).astype(jnp.bfloat16)
    values = jnp.dot(hidden_units, second_weight, preferred_element_type=jnp.float32)
    scaled = values * lax.rsqrt(lax.optimization_barrier(jnp.mean(values * values, axis=-1, keepdims=True)) + 1e-06)
    return scaled.astype(jnp.bfloat16).reshape(count_tiles, pixels, -1)

def silu_slope(pre_act):
    sigmoid = jax.nn.sigmoid(pre_act)
    return sigmoid * (1.0 + pre_act * (1.0 - sigmoid))

def reference(voxels, conv_first, conv_second, head_weight, teacher_in, teacher_out, tile_feats, interpolation, tile_lists):
    first_matrix = conv_first.reshape(-1, CH)
    second_matrix = conv_second.reshape(-1, CH)
    flip_matrix = conv_second.transpose(0, 2, 1).reshape(-1, CH)
    hidden = jax.nn.silu(convolve(voxels, first_matrix, False)).astype(jnp.bfloat16)
    pre_second = convolve(hidden, second_matrix, False)
    second_out = (hidden.astype(jnp.float32) + jax.nn.silu(pre_second)).astype(jnp.bfloat16)
    pred_full = jnp.dot(second_out.reshape(-1, CH), head_weight, preferred_element_type=jnp.float32)
    prediction = pred_full.astype(jnp.bfloat16).reshape(VX, VY, VZ, DT)
    features = teacher_features(tile_feats, teacher_in, teacher_out)
    half_z = BRICK // 2

    def one_device(flat_index):
        index_x = flat_index // (N_GY * N_GZ)
        index_y = flat_index // N_GZ % N_GY
        index_z = flat_index % N_GZ
        chosen = tile_lists[index_x, index_y, index_z]
        picked = features[chosen]
        interp_rows = lax.dynamic_slice_in_dim(interpolation, index_z % 2 * half_z, half_z, 3)
        return jnp.einsum('kxyzp,kpd->xyzd', interp_rows.astype(jnp.float32), picked.astype(jnp.float32))
    blocks = lax.map(one_device, jnp.arange(N_GX * N_GY * N_GZ, dtype=jnp.int32))
    blocks = blocks.reshape(N_GX, N_GY, N_GZ, BRICK, BRICK, half_z, DT)
    target = blocks.transpose(0, 3, 1, 4, 2, 5, 6).reshape(-1, DT)
    residual_pred = (pred_full - target).astype(jnp.bfloat16)
    grad_second = jnp.dot(residual_pred, head_weight.T, preferred_element_type=jnp.float32).reshape(VX, VY, VZ, CH)
    gate_grad = (grad_second * silu_slope(pre_second)).astype(jnp.bfloat16)
    back_term = convolve(gate_grad, flip_matrix, True)
    hidden_grad = (grad_second + back_term).astype(jnp.bfloat16)
    return (prediction, hidden_grad)
```

```python
import functools

import jax
import jax.numpy as jnp
import numpy as np
from jax import lax
from jax.experimental import pallas as pl
from jax.experimental.pallas import tpu as pltpu
from jax.sharding import PartitionSpec as P

MESH = pl.DeviceIdType.MESH
BF = jnp.bfloat16
F32 = jnp.float32
NT = (((1,), (1,)), ((), ()))

SECTIONS = (
    (0, -1, 0, 64),
    (0, 1, 64, 64),
    (-1, 0, 128, 32),
    (1, 0, 160, 32),
    (-1, -1, 192, 16),
    (-1, 1, 208, 16),
    (1, -1, 224, 16),
    (1, 1, 240, 16),
)


def source_row(x, y, z):
    dy = -1 if y < 0 else (1 if y > 7 else 0)
    dz = -1 if z < 0 else (1 if z > 3 else 0)
    if dy == 0 and dz == 0:
        return x * 32 + y * 4 + z
    for sy, sz, first, _ in SECTIONS:
        if (sy, sz) == (dy, dz):
            if dy == 0:
                return 256 + first + x * 8 + y
            if dz == 0:
                return 256 + first + x * 4 + z
            return 256 + first + x


def tables():
    shift = np.zeros((9, 256, 512), np.float32)
    for dy in range(3):
        for dz in range(3):
            for x in range(8):
                for y in range(8):
                    for z in range(4):
                        shift[dy * 3 + dz, x * 32 + y * 4 + z, source_row(x, y + dy - 1, z + dz - 1)] = 1
    stage = np.zeros((256, 256), np.float32)
    for sy, sz, first, _ in SECTIONS:
        ys = range(8) if sy == 0 else ([7] if sy < 0 else [0])
        zs = range(4) if sz == 0 else ([3] if sz < 0 else [0])
        for x in range(8):
            for y in ys:
                for z in zs:
                    if sy == 0:
                        row = first + x * 8 + y
                    elif sz == 0:
                        row = first + x * 4 + z
                    else:
                        row = first + x
                    stage[row, x * 32 + y * 4 + z] = 1
    plane = np.zeros((128, 512), np.float32)
    for side, x in ((0, 7), (1, 0)):
        for y in range(-1, 9):
            for z in range(-1, 5):
                plane[side * 64 + (y + 1) * 6 + z + 1, source_row(x, y, z)] = 1
    spread = np.zeros((288, 64), np.float32)
    for dy in range(3):
        for dz in range(3):
            for y in range(8):
                for z in range(4):
                    spread[(dy * 3 + dz) * 32 + y * 4 + z, (y + dy) * 6 + z + dz] = 1
    halves = np.zeros((512, 512), np.float32)
    for h in range(2):
        for uv in range(64):
            for w in range(4):
                halves[h * 256 + uv * 4 + w, uv * 8 + h * 4 + w] = 1
    return [jnp.asarray(t, BF) for t in (shift, stage, plane, spread, halves)]


def dot(a, b):
    return jnp.dot(a, b, preferred_element_type=F32)


def dot_nt(a, b):
    return lax.dot_general(a, b, NT, preferred_element_type=F32)


def kernel(
    blob, tiles, lists_in, voxels, head, interp, shift, stage, plane, spread, halves,
    pred_out, grad_out,
    G, R, A, B, F, IR, IP, FE, TS, TR, FA, S, SX, XR, P9, LV, LS, HP, ACC, PRE, GS, SO, PP,
    loc, zr, zs, ir, isn, sbs, sbr, l1s, l1r, l2s, l2r, a1s, a1r, a2s, a2r, hs, hr, xs, xr, ts, tr,
):
    gx, gy, gz = lax.axis_index("gx"), lax.axis_index("gy"), lax.axis_index("gz")
    cx, cy, core = gy, gz // 2, gz % 2
    sib = gz + 1 - 2 * core

    def chip(x, y, c):
        return (gx, x % 4, (y % 4) * 2 + c)

    def remote(src, dst, ss, rs, dev):
        return pltpu.make_async_remote_copy(
            src_ref=src, dst_ref=dst, send_sem=ss, recv_sem=rs, device_id=dev, device_id_type=MESH
        )

    def bytes_of(ref, sem):
        return pltpu.make_async_copy(ref, ref, sem)

    along = cy + core * (cx - cy)

    def weight_peer(k):
        return chip(cx + k * core, cy + k * (1 - core), core)

    first = cx + core * (cy - cx)
    second = cy + core * (cx - cy)

    def tile_peer(f, s, c):
        return chip(f + core * (s - f), s + core * (f - s), c)

    lanes = pl.ds(pl.multiple_of(core * 128, 128), 128)
    wide = pl.ds(pl.multiple_of(core * 256, 256), 256)
    quarter = pl.ds(along * 9, 9)

    def rows16(zb):
        return pl.ds(pl.multiple_of(zb * 16, 16), 16)

    barrier = pltpu.get_barrier_semaphore()
    partners = [((gx + 1) % 16, gy, gz), ((gx + 15) % 16, gy, gz)]
    partners += [(gx, (gy + k) % 4, gz) for k in (1, 2, 3)]
    partners += [(gx, gy, (gz + k) % 8) for k in range(1, 8)]
    partners += [(gx, (gy + i) % 4, (gz + j) % 8) for i in (1, 3) for j in (1, 7)]
    partners += [(gx, (gy + 2) % 4, sib)]
    for dev in partners:
        pl.semaphore_signal(barrier, inc=1, device_id=dev, device_id_type=MESH)

    own_w = pltpu.make_async_copy(
        blob.at[:, quarter, :, lanes], G.at[:, quarter, rows16(gx), lanes], loc.at[0]
    )
    own_w.start()
    pixels = pl.ds(pl.multiple_of((first * 4 + second) * 16, 16), 16)
    own_r = pltpu.make_async_copy(tiles.at[:, pixels, wide], R.at[pl.ds(gx * 4, 4)], loc.at[1])
    own_r.start()
    own_i = pltpu.make_async_copy(interp.at[pl.ds(core * 4, 4)], IR, loc.at[2])
    own_i.start()
    LV[cx, cy] = lists_in[...]

    def exists(dy, dz):
        y, z = gy + dy, gz + dz
        return (y >= 0) & (y < 4) & (z >= 0) & (z < 8)

    for dy, dz, at, rows in SECTIONS:

        @pl.when(jnp.logical_not(exists(dy, dz)))
        def _():
            for e in range(3):
                FA[e, 256 + at : 256 + at + rows] = jnp.zeros((rows, 256), BF)

    for side, there in ((0, gx > 0), (1, gx < 15)):

        @pl.when(jnp.logical_not(there))
        def _():
            for e in range(3):
                XR[e, side * 64 : side * 64 + 64] = jnp.zeros((64, 256), BF)

    def halo_copy(e, k):
        dy, dz, at, rows = SECTIONS[k]
        return remote(
            S.at[e, pl.ds(at, rows)], FA.at[e, pl.ds(256 + at, rows)], hs.at[e, k], hr.at[e, k],
            (gx, (gy - dy + 4) % 4, (gz - dz + 8) % 8),
        )

    def halo_stage(e, value):
        FA[e, 0:256] = value
        S[e] = dot(stage[...], value).astype(BF)

    def halo_send(e):
        for k, (dy, dz, _, _) in enumerate(SECTIONS):

            @pl.when(exists(-dy, -dz))
            def _():
                halo_copy(e, k).start()

    def plane_copy(e, side):
        return remote(
            SX.at[e, pl.ds(side * 64, 64)], XR.at[e, pl.ds(side * 64, 64)], xs.at[e, side], xr.at[e, side],
            ((gx + 1 - 2 * side + 16) % 16, gy, gz),
        )

    def halo_middle(e):
        for k, (dy, dz, _, _) in enumerate(SECTIONS):

            @pl.when(exists(dy, dz))
            def _():
                halo_copy(e, k).wait_recv()

            @pl.when(exists(-dy, -dz))
            def _():
                halo_copy(e, k).wait_send()

        SX[e] = dot(plane[...], FA[e]).astype(BF)
        for side, there in ((0, gx < 15), (1, gx > 0)):

            @pl.when(there)
            def _():
                plane_copy(e, side).start()

        def one(j, _):
            P9[j, 1:9] = dot(shift[j], FA[e]).astype(BF).reshape(8, 32, 256)
            return 0

        lax.fori_loop(0, 9, one, 0)

    def halo_end(e):
        for side in range(2):
            came = (gx > 0) if side == 0 else (gx < 15)
            went = (gx < 15) if side == 0 else (gx > 0)

            @pl.when(came)
            def _():
                plane_copy(e, side).wait_recv()

            @pl.when(went)
            def _():
                plane_copy(e, side).wait_send()

            spread_rows = dot(spread[...], XR[e, side * 64 : side * 64 + 64]).astype(BF)
            P9[:, 9 * side] = spread_rows.reshape(9, 32, 256)

    def block(i):
        return G[i // 36, i % 36]

    def convolve(base):
        ACC[...] = jnp.zeros_like(ACC)

        def one(j, _):
            total = ACC[...]
            for dx in range(3):
                total += dot_nt(P9[j, dx : dx + 8].reshape(256, 256), block(base + dx * 9 + j))
            ACC[...] = total
            return 0

        lax.fori_loop(0, 9, one, 0)

    def convolve_back(base):
        ACC[...] = jnp.zeros_like(ACC)

        def one(j, _):
            total = ACC[...]
            for dx in range(3):
                total += dot(P9[8 - j, 2 - dx : 10 - dx].reshape(256, 256), block(base + dx * 9 + j))
            ACC[...] = total
            return 0

        lax.fori_loop(0, 9, one, 0)

    halo_stage(0, voxels[...])
    own_w.wait()
    own_r.wait()
    pl.semaphore_wait(barrier, len(partners))

    def z_of(d, t):
        return (gx + 32 - t) % 16 if d == 0 else (gx + t) % 16

    def ring_copy(kind, d, t):
        zb = z_of(d, t)
        ref = R.at[pl.ds(zb * 4, 4)] if kind == 0 else G.at[kind - 1, quarter, rows16(zb), lanes]
        dev = ((gx + (1 if d == 0 else 15)) % 16, gy, gz)
        return remote(ref, ref, zs.at[kind], zr.at[kind, d, t + 1], dev)

    def ring_wait(kind, d, t):
        zb = z_of(d, t)
        ref = R.at[pl.ds(zb * 4, 4)] if kind == 0 else G.at[kind - 1, quarter, rows16(zb), lanes]
        bytes_of(ref, zr.at[kind, d, t]).wait()

    def piece(q, zb):
        return G.at[:, pl.ds((q % 4) * 9, 9), rows16(zb), lanes]

    def spread_copy(k, d, t):
        ref = piece(along, z_of(d, t))
        return remote(ref, ref, isn, ir.at[k - 1, d, t], weight_peer(k))

    def sibling_copy(q, d, t):
        ref = piece(q, z_of(d, t))
        return remote(ref, ref, sbs, sbr, (gx, gy, sib))

    def hand_out(d, t):
        for k in (1, 3, 2):
            spread_copy(k, d, t).start()
        sibling_copy(along, d, t).start()

    def take_in(d, t):
        for k in (1, 3, 2):
            bytes_of(piece(along + 4 - k, z_of(d, t)), ir.at[k - 1, d, t]).wait()
            sibling_copy(along + 4 - k, d, t).start()

    def list_first(k):
        return remote(lists_in, LV.at[cx, cy], l1s.at[k - 1], l1r.at[k - 1], (gx, (gy + k) % 4, gz))

    def list_second(k):
        ref = LV.at[:, cy]
        return remote(ref, ref, l2s.at[k - 1], l2r.at[k - 1], (gx, gy, (gz + 2 * k) % 8))

    for kind in range(3):
        for d in range(2):
            ring_copy(kind, d, 0).start()
    halo_send(0)
    for k in (1, 2, 3):
        list_first(k).start()
    hand_out(0, 0)

    def ring_step(t, _):
        for kind in range(3):
            for d in range(2):
                ring_wait(kind, d, t)
                if d == 0:
                    ring_copy(kind, d, t).start()
                else:

                    @pl.when(t < 7)
                    def _():
                        ring_copy(kind, d, t).start()

        for d in range(2):
            hand_out(d, t)

        @pl.when(t == 1)
        def _():
            take_in(0, 0)

        @pl.when(t > 1)
        def _():
            for d in range(2):
                take_in(d, t - 1)

        return 0

    lax.fori_loop(1, 3, ring_step, 0)
    for k in (1, 2, 3):
        bytes_of(LV.at[(cx + 4 - k) % 4, cy], l1r.at[k - 1]).wait()
        list_first(k).wait_send()
    for k in (1, 2, 3):
        list_second(k).start()
    halo_middle(0)
    column = lax.broadcasted_iota(jnp.int32, (768, 768), 1)
    natural = ((column & 255) >> 4) * 48 + (column >> 8) * 16 + (column & 15)
    order = (lax.broadcasted_iota(jnp.int32, (768, 768), 0) == natural).astype(BF)
    HP[...] = dot(head[...], order).astype(BF)
    lax.fori_loop(3, 5, ring_step, 0)
    halo_end(0)
    for k in (1, 2, 3):
        bytes_of(LV.at[:, (cy + 4 - k) % 4], l2r.at[k - 1]).wait()
        list_second(k).wait_send()
    to_smem = pltpu.make_async_copy(LV, LS, loc.at[3])
    to_smem.start()
    own_i.wait()

    def reorder(s, _):
        IP[s] = dot(halves[...], IR[s]).astype(BF)
        return 0

    lax.fori_loop(0, 4, reorder, 0)
    to_smem.wait()
    lax.fori_loop(5, 8, ring_step, 0)

    ring_wait(0, 0, 8)

    def first_copy(k):
        return remote(A.at[k - 1], B.at[:, :, first], a1s.at[k - 1], a1r.at[k - 1], tile_peer((first + k) % 4, second, core))

    def pick(k):
        f = (first + k) % 4

        def one(n, _):
            s = n // 8
            x = f + core * (s - f)
            y = s + core * (f - s)
            tile = R[LS[x, y, gx, n % 8]]
            if k == 0:
                B[s, n % 8, first] = tile
            else:
                A[k - 1, s, n % 8] = tile
            return 0

        lax.fori_loop(0, 32, one, 0)

    for k in (2, 1, 3):
        pick(k)
        first_copy(k).start()
    for kind in (1, 2):
        ring_wait(kind, 0, 8)
    hand_out(0, 8)
    for d in range(2):
        take_in(d, 7)
    pick(0)
    take_in(0, 8)
    half = G.at[:, :, :, lanes]
    other = G.at[:, :, :, pl.ds(pl.multiple_of((1 - core) * 128, 128), 128)]
    bytes_of(other, sbr).wait()

    convolve(0)
    pre = ACC[...]
    hidden = (pre * jax.nn.sigmoid(pre)).astype(BF)
    halo_stage(1, hidden)
    halo_send(1)

    for k in (1, 2, 3):
        bytes_of(B.at[:, :, (first + 4 - k) % 4], a1r.at[k - 1]).wait()

    def second_copy(k, flip):
        c = core + flip * (1 - 2 * core)
        s = (second + k) % 4
        return remote(
            B.at[s, pl.ds(c * 4, 4)], F.at[core, :, :, second], a2s.at[k, flip], a2r.at[k, flip], tile_peer(first, s, c)
        )

    stay = pltpu.make_async_copy(B.at[second, pl.ds(core * 4, 4)], F.at[core, :, :, second], loc.at[4])
    for k, flip in ((2, 0), (2, 1), (1, 0), (1, 1), (3, 0), (3, 1), (0, 1)):
        second_copy(k, flip).start()
    stay.start()

    halo_middle(1)
    halo_end(1)
    convolve(42)
    pre = ACC[...]
    PRE[...] = pre
    SO[...] = (FA[1, 0:256].astype(F32) + pre * jax.nn.sigmoid(pre)).astype(BF)

    def head_part(n, _):
        cols = pl.ds(pl.multiple_of(n * 256, 256), 256)
        pred_out[:, cols] = dot(SO[...], head[:, cols]).astype(BF)
        PP[:, cols] = dot(SO[...], HP[:, cols])
        return 0

    lax.fori_loop(0, 3, head_part, 0)

    stay.wait()
    bytes_of(F.at[core, :, :, 0], a2r.at[0, 1]).wait()
    for k in (1, 2, 3):
        for flip in range(2):
            bytes_of(F.at[core, :, :, 0], a2r.at[k, flip]).wait()

    def teach(s, _):
        left = F[0, s].reshape(256, 256)
        right = F[1, s].reshape(256, 256)
        units = []
        for a in range(3):
            raw = dot_nt(left, block(27 + 2 * a)) + dot_nt(right, block(28 + 2 * a))
            units.append((raw * jax.nn.sigmoid(raw)).astype(BF))
        values = []
        for a in range(3):
            part = dot_nt(units[0], block(33 + 3 * a))
            part += dot_nt(units[1], block(34 + 3 * a))
            part += dot_nt(units[2], block(35 + 3 * a))
            values.append(part)
        power = sum(jnp.sum(v * v, axis=1, keepdims=True) for v in values)
        scale = lax.rsqrt(power * (1.0 / 768.0) + 1e-6)
        for a in range(3):
            FE[s, :, a * 256 : (a + 1) * 256] = (values[a] * scale).astype(BF)
        return 0

    lax.fori_loop(0, 4, teach, 0)

    def target(h, into):
        rows = pl.ds(pl.multiple_of(h * 256, 256), 256)

        def one(n, _):
            cols = pl.ds(pl.multiple_of(n * 256, 256), 256)
            total = dot(IP[0, rows], FE[0, :, cols])
            for s in range(1, 4):
                total += dot(IP[s, rows], FE[s, :, cols])
            into(cols, total)
            return 0

        lax.fori_loop(0, 3, one, 0)

    def to_send(cols, total):
        TS[:, cols] = total

    def to_own(cols, total):
        PP[:, cols] = PP[:, cols] - total

    target(1 - core, to_send)
    swap = remote(TS, TR, ts, tr, (gx, gy, sib))
    swap.start()
    target(core, to_own)
    swap.wait()
    residual = (PP[...] - TR[...]).astype(BF)
    back = dot_nt(residual, HP[...])
    GS[...] = back
    pre = PRE[...]
    gate = jax.nn.sigmoid(pre)
    halo_stage(2, (back * (gate * (1.0 + pre * (1.0 - gate)))).astype(BF))
    halo_send(2)
    halo_middle(2)
    halo_end(2)
    convolve_back(42)
    grad_out[...] = (GS[...] + ACC[...]).astype(BF)

    bytes_of(R.at[pl.ds(0, 60)], zs.at[0]).wait()
    for kind in (1, 2):
        bytes_of(G.at[kind - 1, pl.ds(0, 9), pl.ds(0, 240), lanes], zs.at[kind]).wait()
    bytes_of(G.at[:, pl.ds(0, 27), :, lanes], isn).wait()
    bytes_of(half, sbs).wait()
    for k in (1, 2, 3):
        first_copy(k).wait_send()
    for k, flip in ((2, 0), (2, 1), (1, 0), (1, 1), (3, 0), (3, 1), (0, 1)):
        second_copy(k, flip).wait_send()


def local(voxels, conv_first, conv_second, head_weight, teacher_in, teacher_out, tile_feats, interpolation, tile_lists):
    first = conv_first.transpose(0, 2, 1)
    second = conv_second.transpose(0, 2, 1)
    t_in = teacher_in.reshape(2, 256, 3, 16).transpose(2, 0, 3, 1).reshape(6, 16, 256)
    t_out = teacher_out.reshape(16, 3, 16, 3, 16).transpose(3, 1, 4, 0, 2).reshape(9, 16, 256)
    blob = jnp.concatenate([first, t_in, t_out, second, jnp.zeros((3, 16, 256), BF)], axis=0)
    blob = blob.reshape(2, 36, 16, 256)
    lists = jnp.pad(tile_lists.reshape(16, 8), ((0, 0), (0, 120)))
    V = pltpu.VMEM
    D = pltpu.SemaphoreType.DMA
    scratch = [
        V((2, 36, 256, 256), BF),
        V((64, 16, 256), BF),
        V((3, 4, 8, 16, 256), BF),
        V((4, 8, 4, 16, 256), BF),
        V((2, 4, 4, 4, 16, 256), BF),
        V((4, 512, 256), BF),
        V((4, 512, 256), BF),
        V((4, 256, 768), BF),
        V((256, 768), F32),
        V((256, 768), F32),
        V((3, 512, 256), BF),
        V((3, 256, 256), BF),
        V((3, 128, 256), BF),
        V((3, 128, 256), BF),
        V((9, 10, 32, 256), BF),
        V((4, 4, 16, 128), jnp.int32),
        pltpu.SMEM((4, 4, 16, 128), jnp.int32),
        V((256, 768), BF),
        V((256, 256), F32),
        V((256, 256), F32),
        V((256, 256), F32),
        V((256, 256), BF),
        V((256, 768), F32),
        D((5,)),
        D((3, 2, 9)), D((3,)),
        D((3, 2, 9)), D,
        D, D,
        D((3,)), D((3,)), D((3,)), D((3,)),
        D((3,)), D((3,)), D((4, 2)), D((4, 2)),
        D((3, 8)), D((3, 8)), D((3, 2)), D((3, 2)),
        D, D,
    ]
    vm = pl.BlockSpec(memory_space=pltpu.VMEM)
    hbm = pl.BlockSpec(memory_space=pl.ANY)
    prediction, hidden_grad = pl.pallas_call(
        kernel,
        out_shape=(jax.ShapeDtypeStruct((256, 768), BF), jax.ShapeDtypeStruct((256, 256), BF)),
        in_specs=[hbm, hbm, vm, vm, vm, hbm, vm, vm, vm, vm, vm],
        out_specs=(vm, vm),
        scratch_shapes=scratch,
        compiler_params=pltpu.CompilerParams(
            collective_id=0, has_side_effects=True, vmem_limit_bytes=56 * 1024 * 1024
        ),
        cost_estimate=pl.CostEstimate(flops=6_000_000_000, bytes_accessed=10_000_000, transcendentals=1_000_000),
    )(
        blob, tile_feats, lists, voxels.reshape(256, 256), head_weight, interpolation.reshape(8, 512, 256), *tables()
    )
    return prediction.reshape(8, 8, 4, 768), hidden_grad.reshape(8, 8, 4, 256)


def solution(mesh):
    in_specs = (
        P("gx", "gy", "gz", None),
        P(None, None, "gx"),
        P(None, None, "gx"),
        P(),
        P(None, "gx"),
        P(None, "gx"),
        P("gx", None, None),
        P(),
        P(None, "gy", "gz", None),
    )
    out_specs = (P("gx", "gy", "gz", None), P("gx", "gy", "gz", None))
    return jax.shard_map(local, mesh=mesh, in_specs=in_specs, out_specs=out_specs, check_vma=False)
```

```python
import functools

import jax
import jax.numpy as jnp
import numpy as np
from jax import lax
from jax.experimental import pallas as pl
from jax.experimental.pallas import tpu as pltpu
from jax.sharding import PartitionSpec as P

MESH = pl.DeviceIdType.MESH
BF = jnp.bfloat16
F32 = jnp.float32
NT = (((1,), (1,)), ((), ()))

SECTIONS = (
    (0, -1, 0, 64),
    (0, 1, 64, 64),
    (-1, 0, 128, 32),
    (1, 0, 160, 32),
    (-1, -1, 192, 16),
    (-1, 1, 208, 16),
    (1, -1, 224, 16),
    (1, 1, 240, 16),
)


def source_row(x, y, z):
    dy = -1 if y < 0 else (1 if y > 7 else 0)
    dz = -1 if z < 0 else (1 if z > 3 else 0)
    if dy == 0 and dz == 0:
        return x * 32 + y * 4 + z
    for sy, sz, first, _ in SECTIONS:
        if (sy, sz) == (dy, dz):
            if dy == 0:
                return 256 + first + x * 8 + y
            if dz == 0:
                return 256 + first + x * 4 + z
            return 256 + first + x


def tables():
    shift = np.zeros((9, 256, 512), np.float32)
    for dy in range(3):
        for dz in range(3):
            for x in range(8):
                for y in range(8):
                    for z in range(4):
                        shift[dy * 3 + dz, x * 32 + y * 4 + z, source_row(x, y + dy - 1, z + dz - 1)] = 1
    stage = np.zeros((256, 256), np.float32)
    for sy, sz, first, _ in SECTIONS:
        ys = range(8) if sy == 0 else ([7] if sy < 0 else [0])
        zs = range(4) if sz == 0 else ([3] if sz < 0 else [0])
        for x in range(8):
            for y in ys:
                for z in zs:
                    if sy == 0:
                        row = first + x * 8 + y
                    elif sz == 0:
                        row = first + x * 4 + z
                    else:
                        row = first + x
                    stage[row, x * 32 + y * 4 + z] = 1
    plane = np.zeros((128, 512), np.float32)
    for side, x in ((0, 7), (1, 0)):
        for y in range(-1, 9):
            for z in range(-1, 5):
                plane[side * 64 + (y + 1) * 6 + z + 1, source_row(x, y, z)] = 1
    spread = np.zeros((288, 64), np.float32)
    for dy in range(3):
        for dz in range(3):
            for y in range(8):
                for z in range(4):
                    spread[(dy * 3 + dz) * 32 + y * 4 + z, (y + dy) * 6 + z + dz] = 1
    halves = np.zeros((512, 512), np.float32)
    for h in range(2):
        for uv in range(64):
            for w in range(4):
                halves[h * 256 + uv * 4 + w, uv * 8 + h * 4 + w] = 1
    return [jnp.asarray(t, BF) for t in (shift, stage, plane, spread, halves)]


def dot(a, b):
    return jnp.dot(a, b, preferred_element_type=F32)


def dot_nt(a, b):
    return lax.dot_general(a, b, NT, preferred_element_type=F32)


def kernel(
    blob, tiles, lists_in, voxels, head, interp, shift, stage, plane, spread, halves,
    pred_out, grad_out,
    G, R, A, B, F, IR, IP, FE, TS, TR, FA, S, SX, XR, P9, LV, LS, HP, ACC, PRE, GS, SO, PP,
    loc, zr, zs, ir, isn, sbs, sbr, l1s, l1r, l2s, l2r, a1s, a1r, a2s, a2r, hs, hr, xs, xr, ts, tr,
):
    gx, gy, gz = lax.axis_index("gx"), lax.axis_index("gy"), lax.axis_index("gz")
    cx, cy, core = gy, gz // 2, gz % 2
    sib = gz + 1 - 2 * core

    def chip(x, y, c):
        return (gx, x % 4, (y % 4) * 2 + c)

    def remote(src, dst, ss, rs, dev):
        return pltpu.make_async_remote_copy(
            src_ref=src, dst_ref=dst, send_sem=ss, recv_sem=rs, device_id=dev, device_id_type=MESH
        )

    def bytes_of(ref, sem):
        return pltpu.make_async_copy(ref, ref, sem)

    along = cy + core * (cx - cy)

    def weight_peer(k):
        return chip(cx + k * core, cy + k * (1 - core), core)

    first = cx + core * (cy - cx)
    second = cy + core * (cx - cy)

    def tile_peer(f, s, c):
        return chip(f + core * (s - f), s + core * (f - s), c)

    lanes = pl.ds(pl.multiple_of(core * 128, 128), 128)
    wide = pl.ds(pl.multiple_of(core * 256, 256), 256)
    barrier = pltpu.get_barrier_semaphore()
    partners = [((gx + k) % 16, gy, gz) for k in (1, 15)]
    partners += [(gx, (gy + k) % 4, gz) for k in (1, 2, 3)]
    partners += [(gx, gy, (gz + k) % 8) for k in range(1, 8)]
    partners += [(gx, (gy + i) % 4, (gz + j) % 8) for i in (1, 3) for j in (1, 7)]
    partners += [(gx, (gy + 2) % 4, sib)]
    for dev in partners:
        pl.semaphore_signal(barrier, inc=1, device_id=dev, device_id_type=MESH)

    own_w = pltpu.make_async_copy(blob.at[along, :, :, lanes], G.at[along, core, gx], loc.at[0])
    own_w.start()
    pixels = pl.ds(pl.multiple_of((first * 4 + second) * 16, 16), 16)
    own_r = pltpu.make_async_copy(tiles.at[:, pixels, wide], R.at[pl.ds(gx * 4, 4)], loc.at[1])
    own_r.start()
    own_i = pltpu.make_async_copy(interp.at[pl.ds(core * 4, 4)], IR, loc.at[2])
    own_i.start()
    LV[cx, cy] = lists_in[...]

    def exists(dy, dz):
        y, z = gy + dy, gz + dz
        return (y >= 0) & (y < 4) & (z >= 0) & (z < 8)

    for dy, dz, at, rows in SECTIONS:

        @pl.when(jnp.logical_not(exists(dy, dz)))
        def _():
            for e in range(3):
                FA[e, 256 + at : 256 + at + rows] = jnp.zeros((rows, 256), BF)

    for side, there in ((0, gx > 0), (1, gx < 15)):

        @pl.when(jnp.logical_not(there))
        def _():
            for e in range(3):
                XR[e, side * 64 : side * 64 + 64] = jnp.zeros((64, 256), BF)

    def halo_copy(e, k):
        dy, dz, at, rows = SECTIONS[k]
        return remote(
            S.at[e, pl.ds(at, rows)], FA.at[e, pl.ds(256 + at, rows)], hs.at[e, k], hr.at[e, k],
            (gx, (gy - dy + 4) % 4, (gz - dz + 8) % 8),
        )

    def halo_stage(e, value):
        FA[e, 0:256] = value
        S[e] = dot(stage[...], value).astype(BF)

    def halo_send(e):
        for k, (dy, dz, _, _) in enumerate(SECTIONS):

            @pl.when(exists(-dy, -dz))
            def _():
                halo_copy(e, k).start()

    def plane_copy(e, side):
        return remote(
            SX.at[e, pl.ds(side * 64, 64)], XR.at[e, pl.ds(side * 64, 64)], xs.at[e, side], xr.at[e, side],
            ((gx + 1 - 2 * side + 16) % 16, gy, gz),
        )

    def halo_middle(e):
        for k, (dy, dz, _, _) in enumerate(SECTIONS):

            @pl.when(exists(dy, dz))
            def _():
                halo_copy(e, k).wait_recv()

            @pl.when(exists(-dy, -dz))
            def _():
                halo_copy(e, k).wait_send()

        SX[e] = dot(plane[...], FA[e]).astype(BF)
        for side, there in ((0, gx < 15), (1, gx > 0)):

            @pl.when(there)
            def _():
                plane_copy(e, side).start()

        def one(j, _):
            P9[j, 1:9] = dot(shift[j], FA[e]).astype(BF).reshape(8, 32, 256)
            return 0

        lax.fori_loop(0, 9, one, 0)

    def halo_end(e):
        for side in range(2):
            came = (gx > 0) if side == 0 else (gx < 15)
            went = (gx < 15) if side == 0 else (gx > 0)

            @pl.when(came)
            def _():
                plane_copy(e, side).wait_recv()

            @pl.when(went)
            def _():
                plane_copy(e, side).wait_send()

            spread_rows = dot(spread[...], XR[e, side * 64 : side * 64 + 64]).astype(BF)
            P9[:, 9 * side] = spread_rows.reshape(9, 32, 256)

    def block(i):
        parts = [G[i // 11, h, :, i % 11].reshape(256, 128) for h in range(2)]
        return jnp.concatenate(parts, axis=1)

    def block_second(i):
        parts = [G[i // 7, h, :, 11 + i % 7].reshape(256, 128) for h in range(2)]
        return jnp.concatenate(parts, axis=1)

    def convolve_middle(blocks, back):
        def one(j, total):
            rows = P9[8 - j if back else j, 1:9].reshape(256, 256)
            return total + (dot if back else dot_nt)(rows, blocks(9 + j))

        ACC[...] = jnp.zeros_like(ACC)

        def three(i, _):
            total = ACC[...]
            for m in range(3):
                total = one(3 * i + m, total)
            ACC[...] = total
            return 0

        lax.fori_loop(0, 3, three, 0)

    def convolve_sides(blocks, back):
        def one(j, _):
            total = ACC[...]
            for dx in (0, 2):
                if back:
                    total += dot(P9[8 - j, 2 - dx : 10 - dx].reshape(256, 256), blocks(dx * 9 + j))
                else:
                    total += dot_nt(P9[j, dx : dx + 8].reshape(256, 256), blocks(dx * 9 + j))
            ACC[...] = total
            return 0

        lax.fori_loop(0, 9, one, 0)

    halo_stage(0, voxels[...])
    own_w.wait()
    own_r.wait()
    pl.semaphore_wait(barrier, len(partners))

    def z_of(d, t):
        return (gx + 32 - t) % 16 if d == 0 else (gx + t) % 16

    limit = (8, 7)

    def ring_piece(kind, d, t):
        zb = z_of(d, t)
        if kind == 0:
            return R.at[pl.ds(zb * 4, 4)]
        return G.at[along, core, zb, pl.ds(0, 11) if kind == 1 else pl.ds(11, 7)]

    def ring_copy(kind, d, t):
        ref = ring_piece(kind, d, t)
        dev = ((gx + (1 if d == 0 else 15)) % 16, gy, gz)
        return remote(ref, ref, zs.at[kind], zr.at[kind, d, t + 1], dev)

    def ring_wait(kind, d, t):
        bytes_of(ring_piece(kind, d, t), zr.at[kind, d, t]).wait()

    def piece(q, d, t):
        return G.at[q % 4, core, z_of(d, t)]

    def spread_copy(k, d, t):
        ref = piece(along, d, t)
        return remote(ref, ref, isn, ir.at[k - 1, d, t], weight_peer(k))

    def sibling_copy(q, d, t):
        ref = piece(q, d, t)
        return remote(ref, ref, sbs, sbr, (gx, gy, sib))

    def hand_out(d, t):
        for k in (2, 1, 3):
            spread_copy(k, d, t).start()
        sibling_copy(along, d, t).start()

    def take_in(d, t):
        for k in (1, 3, 2):
            bytes_of(piece(along + 4 - k, d, t), ir.at[k - 1, d, t]).wait()
            sibling_copy(along + 4 - k, d, t).start()

    def ring_step(t):
        for kind in range(3):
            for d in range(2):
                if t <= limit[d]:
                    ring_wait(kind, d, t)
                if t < limit[d]:
                    ring_copy(kind, d, t).start()
        for d in range(2):
            if t <= limit[d]:
                hand_out(d, t)

    def take_step(t):
        for d in range(2):
            if t <= limit[d] and (t > 0 or d == 0):
                take_in(d, t)

    def list_first(k):
        return remote(lists_in, LV.at[cx, cy], l1s.at[k - 1], l1r.at[k - 1], (gx, (gy + k) % 4, gz))

    def list_second(k):
        ref = LV.at[:, cy]
        return remote(ref, ref, l2s.at[k - 1], l2r.at[k - 1], (gx, gy, (gz + 2 * k) % 8))

    def first_copy(k):
        return remote(A.at[k - 1], B.at[:, :, first], a1s.at[k - 1], a1r.at[k - 1], tile_peer((first + k) % 4, second, core))

    def pick(k):
        f = (first + k) % 4

        def one(s, _):
            x = f + core * (s - f)
            y = s + core * (f - s)
            for n in range(8):
                tile = R[LS[x, y, gx, n]]
                if k == 0:
                    B[s, n, first] = tile
                else:
                    A[k - 1, s, n] = tile
            return 0

        lax.fori_loop(0, 4, one, 0)

    def second_copy(k, flip):
        c = core + flip * (1 - 2 * core)
        s = (second + k) % 4
        return remote(
            B.at[s, pl.ds(c * 4, 4)], F.at[core, :, :, second], a2s.at[k, flip], a2r.at[k, flip], tile_peer(first, s, c)
        )

    second_all = ((2, 0), (2, 1), (1, 0), (1, 1), (3, 0), (3, 1), (0, 1))

    for kind in range(3):
        for d in range(2):
            ring_copy(kind, d, 0).start()
    for k in (1, 2, 3):
        list_first(k).start()
    halo_send(0)
    hand_out(0, 0)

    ring_step(1)
    ring_step(2)
    take_step(0)
    for k in (1, 2, 3):
        bytes_of(LV.at[(cx + 4 - k) % 4, cy], l1r.at[k - 1]).wait()
        list_first(k).wait_send()
    for k in (1, 2, 3):
        list_second(k).start()
    ring_step(3)
    take_step(1)
    halo_middle(0)
    ring_step(4)
    take_step(2)
    column = lax.broadcasted_iota(jnp.int32, (768, 768), 1)
    natural = ((column & 255) >> 4) * 48 + (column >> 8) * 16 + (column & 15)
    order = (lax.broadcasted_iota(jnp.int32, (768, 768), 0) == natural).astype(BF)
    HP[...] = dot(head[...], order).astype(BF)
    ring_step(5)
    take_step(3)
    for k in (1, 2, 3):
        bytes_of(LV.at[:, (cy + 4 - k) % 4], l2r.at[k - 1]).wait()
        list_second(k).wait_send()
    to_smem = pltpu.make_async_copy(LV, LS, loc.at[3])
    to_smem.start()
    halo_end(0)
    ring_step(6)
    take_step(4)
    own_i.wait()

    def reorder(s, _):
        IP[s] = dot(halves[...], IR[s]).astype(BF)
        return 0

    lax.fori_loop(0, 4, reorder, 0)
    ring_step(7)
    take_step(5)
    to_smem.wait()

    ring_wait(0, 0, 8)
    for k in (2, 1, 3):
        pick(k)
        first_copy(k).start()
    for kind in (1, 2):
        ring_wait(kind, 0, 8)
    hand_out(0, 8)
    take_step(6)
    pick(0)
    take_step(7)
    take_step(8)
    for k in (1, 2, 3):
        bytes_of(B.at[:, :, (first + 4 - k) % 4], a1r.at[k - 1]).wait()
    stay = pltpu.make_async_copy(B.at[second, pl.ds(core * 4, 4)], F.at[core, :, :, second], loc.at[4])
    for k, flip in second_all:
        second_copy(k, flip).start()
    stay.start()
    bytes_of(G.at[:, 1 - core], sbr).wait()

    convolve_middle(block, False)
    convolve_sides(block, False)
    pre = ACC[...]
    hidden = (pre * jax.nn.sigmoid(pre)).astype(BF)
    halo_stage(1, hidden)
    halo_send(1)

    stay.wait()
    for k, flip in second_all:
        bytes_of(F.at[core, :, :, 0], a2r.at[k, flip]).wait()

    def teach(s, _):
        left = F[0, s].reshape(256, 256)
        right = F[1, s].reshape(256, 256)
        units = []
        for a in range(3):
            raw = dot_nt(left, block(27 + 2 * a)) + dot_nt(right, block(28 + 2 * a))
            units.append((raw * jax.nn.sigmoid(raw)).astype(BF))
        values = []
        for a in range(3):
            part = dot_nt(units[0], block(33 + 3 * a))
            part += dot_nt(units[1], block(34 + 3 * a))
            part += dot_nt(units[2], block(35 + 3 * a))
            values.append(part)
        power = sum(jnp.sum(v * v, axis=1, keepdims=True) for v in values)
        scale = lax.rsqrt(power * (1.0 / 768.0) + 1e-6)
        for a in range(3):
            FE[s, :, a * 256 : (a + 1) * 256] = (values[a] * scale).astype(BF)
        return 0

    def target(h, into):
        rows = pl.ds(pl.multiple_of(h * 256, 256), 256)

        def one(n, _):
            cols = pl.ds(pl.multiple_of(n * 256, 256), 256)
            total = dot(IP[0, rows], FE[0, :, cols])
            for s in range(1, 4):
                total += dot(IP[s, rows], FE[s, :, cols])
            into[:, cols] = total
            return 0

        lax.fori_loop(0, 3, one, 0)

    lax.fori_loop(0, 1, teach, 0)
    halo_middle(1)
    lax.fori_loop(1, 3, teach, 0)
    halo_end(1)
    lax.fori_loop(3, 4, teach, 0)
    target(1 - core, TS)
    swap = remote(TS, TR, ts, tr, (gx, gy, sib))
    swap.start()
    target(core, PP)

    convolve_middle(block_second, False)
    convolve_sides(block_second, False)
    pre = ACC[...]
    PRE[...] = pre
    SO[...] = (FA[1, 0:256].astype(F32) + pre * jax.nn.sigmoid(pre)).astype(BF)
    swap.wait()

    def head_part(n, _):
        cols = pl.ds(pl.multiple_of(n * 256, 256), 256)
        PP[:, cols] = dot(SO[...], HP[:, cols]) - (PP[:, cols] + TR[:, cols])
        return 0

    lax.fori_loop(0, 3, head_part, 0)
    back = dot_nt(PP[...].astype(BF), HP[...])
    GS[...] = back
    pre = PRE[...]
    gate = jax.nn.sigmoid(pre)
    halo_stage(2, (back * (gate * (1.0 + pre * (1.0 - gate)))).astype(BF))
    halo_send(2)

    def predict(n, _):
        cols = pl.ds(pl.multiple_of(n * 256, 256), 256)
        pred_out[:, cols] = dot(SO[...], head[:, cols]).astype(BF)
        return 0

    lax.fori_loop(0, 3, predict, 0)
    halo_middle(2)
    convolve_middle(block_second, True)
    halo_end(2)
    convolve_sides(block_second, True)
    grad_out[...] = (GS[...] + ACC[...]).astype(BF)

    bytes_of(R.at[pl.ds(0, 60)], zs.at[0]).wait()
    bytes_of(G.at[along, core, pl.ds(0, 15), pl.ds(0, 11)], zs.at[1]).wait()
    bytes_of(G.at[along, core, pl.ds(0, 15), pl.ds(11, 7)], zs.at[2]).wait()
    bytes_of(G.at[pl.ds(0, 3), core], isn).wait()
    bytes_of(G.at[:, core], sbs).wait()
    for k in (1, 2, 3):
        first_copy(k).wait_send()
    for k, flip in second_all:
        second_copy(k, flip).wait_send()


def local(voxels, conv_first, conv_second, head_weight, teacher_in, teacher_out, tile_feats, interpolation, tile_lists):
    first = conv_first.transpose(0, 2, 1)
    second = conv_second.transpose(0, 2, 1)
    t_in = teacher_in.reshape(2, 256, 3, 16).transpose(2, 0, 3, 1).reshape(6, 16, 256)
    t_out = teacher_out.reshape(16, 3, 16, 3, 16).transpose(3, 1, 4, 0, 2).reshape(9, 16, 256)
    early = jnp.concatenate([first, t_in, t_out, jnp.zeros((2, 16, 256), BF)], axis=0).reshape(4, 11, 16, 256)
    late = jnp.concatenate([second, jnp.zeros((1, 16, 256), BF)], axis=0).reshape(4, 7, 16, 256)
    blob = jnp.concatenate([early, late], axis=1)
    lists = jnp.pad(tile_lists.reshape(16, 8), ((0, 0), (0, 120)))
    V = pltpu.VMEM
    D = pltpu.SemaphoreType.DMA
    scratch = [
        V((4, 2, 16, 18, 16, 128), BF),
        V((64, 16, 256), BF),
        V((3, 4, 8, 16, 256), BF),
        V((4, 8, 4, 16, 256), BF),
        V((2, 4, 4, 4, 16, 256), BF),
        V((4, 512, 256), BF),
        V((4, 512, 256), BF),
        V((4, 256, 768), BF),
        V((256, 768), F32),
        V((256, 768), F32),
        V((3, 512, 256), BF),
        V((3, 256, 256), BF),
        V((3, 128, 256), BF),
        V((3, 128, 256), BF),
        V((9, 10, 32, 256), BF),
        V((4, 4, 16, 128), jnp.int32),
        pltpu.SMEM((4, 4, 16, 128), jnp.int32),
        V((256, 768), BF),
        V((256, 256), F32),
        V((256, 256), F32),
        V((256, 256), F32),
        V((256, 256), BF),
        V((256, 768), F32),
        D((5,)),
        D((3, 2, 9)), D((3,)),
        D((3, 2, 9)), D,
        D, D,
        D((3,)), D((3,)), D((3,)), D((3,)),
        D((3,)), D((3,)), D((4, 2)), D((4, 2)),
        D((3, 8)), D((3, 8)), D((3, 2)), D((3, 2)),
        D, D,
    ]
    vm = pl.BlockSpec(memory_space=pltpu.VMEM)
    hbm = pl.BlockSpec(memory_space=pl.ANY)
    prediction, hidden_grad = pl.pallas_call(
        kernel,
        out_shape=(jax.ShapeDtypeStruct((256, 768), BF), jax.ShapeDtypeStruct((256, 256), BF)),
        in_specs=[hbm, hbm, vm, vm, vm, hbm, vm, vm, vm, vm, vm],
        out_specs=(vm, vm),
        scratch_shapes=scratch,
        compiler_params=pltpu.CompilerParams(
            collective_id=0, has_side_effects=True, vmem_limit_bytes=56 * 1024 * 1024
        ),
        cost_estimate=pl.CostEstimate(flops=6_000_000_000, bytes_accessed=10_000_000, transcendentals=1_000_000),
    )(
        blob, tile_feats, lists, voxels.reshape(256, 256), head_weight, interpolation.reshape(8, 512, 256), *tables()
    )
    return prediction.reshape(8, 8, 4, 768), hidden_grad.reshape(8, 8, 4, 256)


def solution(mesh):
    in_specs = (
        P("gx", "gy", "gz", None),
        P(None, None, "gx"),
        P(None, None, "gx"),
        P(),
        P(None, "gx"),
        P(None, "gx"),
        P("gx", None, None),
        P(),
        P(None, "gy", "gz", None),
    )
    out_specs = (P("gx", "gy", "gz", None), P("gx", "gy", "gz", None))
    return jax.shard_map(local, mesh=mesh, in_specs=in_specs, out_specs=out_specs, check_vma=False)
```

```python
import functools

import jax
import jax.numpy as jnp
import numpy as np
from jax import lax
from jax.experimental import pallas as pl
from jax.experimental.pallas import tpu as pltpu
from jax.sharding import PartitionSpec as P

MESH = pl.DeviceIdType.MESH
BF = jnp.bfloat16
F32 = jnp.float32
NT = (((1,), (1,)), ((), ()))

SECTIONS = (
    (0, -1, 0, 64),
    (0, 1, 64, 64),
    (-1, 0, 128, 32),
    (1, 0, 160, 32),
    (-1, -1, 192, 16),
    (-1, 1, 208, 16),
    (1, -1, 224, 16),
    (1, 1, 240, 16),
)


def source_row(x, y, z):
    dy = -1 if y < 0 else (1 if y > 7 else 0)
    dz = -1 if z < 0 else (1 if z > 3 else 0)
    if dy == 0 and dz == 0:
        return x * 32 + y * 4 + z
    for sy, sz, first, _ in SECTIONS:
        if (sy, sz) == (dy, dz):
            if dy == 0:
                return 256 + first + x * 8 + y
            if dz == 0:
                return 256 + first + x * 4 + z
            return 256 + first + x


def tables():
    shift = np.zeros((9, 256, 512), np.float32)
    for dy in range(3):
        for dz in range(3):
            for x in range(8):
                for y in range(8):
                    for z in range(4):
                        shift[dy * 3 + dz, x * 32 + y * 4 + z, source_row(x, y + dy - 1, z + dz - 1)] = 1
    stage = np.zeros((256, 256), np.float32)
    for sy, sz, first, _ in SECTIONS:
        ys = range(8) if sy == 0 else ([7] if sy < 0 else [0])
        zs = range(4) if sz == 0 else ([3] if sz < 0 else [0])
        for x in range(8):
            for y in ys:
                for z in zs:
                    if sy == 0:
                        row = first + x * 8 + y
                    elif sz == 0:
                        row = first + x * 4 + z
                    else:
                        row = first + x
                    stage[row, x * 32 + y * 4 + z] = 1
    plane = np.zeros((128, 512), np.float32)
    for side, x in ((0, 7), (1, 0)):
        for y in range(-1, 9):
            for z in range(-1, 5):
                plane[side * 64 + (y + 1) * 6 + z + 1, source_row(x, y, z)] = 1
    spread = np.zeros((288, 64), np.float32)
    for dy in range(3):
        for dz in range(3):
            for y in range(8):
                for z in range(4):
                    spread[(dy * 3 + dz) * 32 + y * 4 + z, (y + dy) * 6 + z + dz] = 1
    halves = np.zeros((512, 512), np.float32)
    for h in range(2):
        for uv in range(64):
            for w in range(4):
                halves[h * 256 + uv * 4 + w, uv * 8 + h * 4 + w] = 1
    return [jnp.asarray(t, BF) for t in (shift, stage, plane, spread, halves)]


def dot(a, b):
    return jnp.dot(a, b, preferred_element_type=F32)


def dot_nt(a, b):
    return lax.dot_general(a, b, NT, preferred_element_type=F32)


def kernel(
    blob, tiles, lists_in, voxels, head, interp, shift_in, stage, plane, spread, halves_in,
    pred_out, grad_out,
    shift, halves, G, R, A, B, F, IR, IP, FE, TS, TR, FA, S, SX, XR, P9, LV, LS, HP, ACC, PRE, GS, SO, PP,
    loc, zr, zs, ir, isn, sbs, sbr, l1s, l1r, l2s, l2r, a1s, a1r, a2s, a2r, hs, hr, xs, xr, ts, tr,
):
    gx, gy, gz = lax.axis_index("gx"), lax.axis_index("gy"), lax.axis_index("gz")
    cx, cy, core = gy, gz // 2, gz % 2
    sib = gz + 1 - 2 * core

    def chip(x, y, c):
        return (gx, x % 4, (y % 4) * 2 + c)

    def remote(src, dst, ss, rs, dev):
        return pltpu.make_async_remote_copy(
            src_ref=src, dst_ref=dst, send_sem=ss, recv_sem=rs, device_id=dev, device_id_type=MESH
        )

    def bytes_of(ref, sem):
        return pltpu.make_async_copy(ref, ref, sem)

    along = cy + core * (cx - cy)

    def weight_peer(k):
        return chip(cx + k * core, cy + k * (1 - core), core)

    first = cx + core * (cy - cx)
    second = cy + core * (cx - cy)

    def tile_peer(f, s, c):
        return chip(f + core * (s - f), s + core * (f - s), c)

    lanes = pl.ds(pl.multiple_of(core * 128, 128), 128)
    wide = pl.ds(pl.multiple_of(core * 256, 256), 256)
    barrier = pltpu.get_barrier_semaphore()
    partners = [((gx + k) % 16, gy, gz) for k in (1, 15)]
    partners += [(gx, (gy + k) % 4, gz) for k in (1, 2, 3)]
    partners += [(gx, gy, (gz + k) % 8) for k in range(1, 8)]
    partners += [(gx, (gy + i) % 4, (gz + j) % 8) for i in (1, 3) for j in (1, 7)]
    partners += [(gx, (gy + 2) % 4, sib)]
    for dev in partners:
        pl.semaphore_signal(barrier, inc=1, device_id=dev, device_id_type=MESH)

    own_w = pltpu.make_async_copy(blob.at[along, :, :, lanes], G.at[along, core, gx], loc.at[0])
    own_w.start()
    pixels = pl.ds(pl.multiple_of((first * 4 + second) * 16, 16), 16)
    own_r = pltpu.make_async_copy(tiles.at[:, pixels, wide], R.at[pl.ds(gx * 4, 4)], loc.at[1])
    own_r.start()
    own_i = pltpu.make_async_copy(interp.at[pl.ds(core * 4, 4)], IR, loc.at[2])
    own_i.start()
    own_s = pltpu.make_async_copy(shift_in, shift, loc.at[5])
    own_s.start()
    own_h = pltpu.make_async_copy(halves_in, halves, loc.at[6])
    own_h.start()
    LV[cx, cy] = lists_in[...]

    def exists(dy, dz):
        y, z = gy + dy, gz + dz
        return (y >= 0) & (y < 4) & (z >= 0) & (z < 8)

    for dy, dz, at, rows in SECTIONS:

        @pl.when(jnp.logical_not(exists(dy, dz)))
        def _():
            for e in range(3):
                FA[e, 256 + at : 256 + at + rows] = jnp.zeros((rows, 256), BF)

    for side, there in ((0, gx > 0), (1, gx < 15)):

        @pl.when(jnp.logical_not(there))
        def _():
            for e in range(3):
                XR[e, side * 64 : side * 64 + 64] = jnp.zeros((64, 256), BF)

    def halo_copy(e, k):
        dy, dz, at, rows = SECTIONS[k]
        return remote(
            S.at[e, pl.ds(at, rows)], FA.at[e, pl.ds(256 + at, rows)], hs.at[e, k], hr.at[e, k],
            (gx, (gy - dy + 4) % 4, (gz - dz + 8) % 8),
        )

    def halo_stage(e, value):
        FA[e, 0:256] = value
        S[e] = dot(stage[...], value).astype(BF)

    def halo_send(e):
        for k, (dy, dz, _, _) in enumerate(SECTIONS):

            @pl.when(exists(-dy, -dz))
            def _():
                halo_copy(e, k).start()

    def plane_copy(e, side):
        return remote(
            SX.at[e, pl.ds(side * 64, 64)], XR.at[e, pl.ds(side * 64, 64)], xs.at[e, side], xr.at[e, side],
            ((gx + 1 - 2 * side + 16) % 16, gy, gz),
        )

    def halo_middle(e):
        for k, (dy, dz, _, _) in enumerate(SECTIONS):

            @pl.when(exists(dy, dz))
            def _():
                halo_copy(e, k).wait_recv()

            @pl.when(exists(-dy, -dz))
            def _():
                halo_copy(e, k).wait_send()

        SX[e] = dot(plane[...], FA[e]).astype(BF)
        for side, there in ((0, gx < 15), (1, gx > 0)):

            @pl.when(there)
            def _():
                plane_copy(e, side).start()

        def one(j, _):
            P9[j, 1:9] = dot(shift[j], FA[e]).astype(BF).reshape(8, 32, 256)
            return 0

        lax.fori_loop(0, 9, one, 0)

    def halo_end(e):
        for side in range(2):
            came = (gx > 0) if side == 0 else (gx < 15)
            went = (gx < 15) if side == 0 else (gx > 0)

            @pl.when(came)
            def _():
                plane_copy(e, side).wait_recv()

            @pl.when(went)
            def _():
                plane_copy(e, side).wait_send()

            spread_rows = dot(spread[...], XR[e, side * 64 : side * 64 + 64]).astype(BF)
            P9[:, 9 * side] = spread_rows.reshape(9, 32, 256)

    def block(i):
        parts = [G[i // 11, h, :, i % 11].reshape(256, 128) for h in range(2)]
        return jnp.concatenate(parts, axis=1)

    def block_second(i):
        parts = [G[i // 7, h, :, 11 + i % 7].reshape(256, 128) for h in range(2)]
        return jnp.concatenate(parts, axis=1)

    def convolve_middle(blocks, back):
        def one(j, total):
            rows = P9[8 - j if back else j, 1:9].reshape(256, 256)
            return total + (dot if back else dot_nt)(rows, blocks(9 + j))

        ACC[...] = jnp.zeros_like(ACC)

        def three(i, _):
            total = ACC[...]
            for m in range(3):
                total = one(3 * i + m, total)
            ACC[...] = total
            return 0

        lax.fori_loop(0, 3, three, 0)

    def convolve_sides(blocks, back):
        def one(j, _):
            total = ACC[...]
            for dx in (0, 2):
                if back:
                    total += dot(P9[8 - j, 2 - dx : 10 - dx].reshape(256, 256), blocks(dx * 9 + j))
                else:
                    total += dot_nt(P9[j, dx : dx + 8].reshape(256, 256), blocks(dx * 9 + j))
            ACC[...] = total
            return 0

        lax.fori_loop(0, 9, one, 0)

    halo_stage(0, voxels[...])
    own_w.wait()
    own_r.wait()
    pl.semaphore_wait(barrier, len(partners))

    def z_of(d, t):
        return (gx + 32 - t) % 16 if d == 0 else (gx + t) % 16

    limit = (8, 7)

    def ring_piece(kind, d, t):
        zb = z_of(d, t)
        if kind == 0:
            return R.at[pl.ds(zb * 4, 4)]
        return G.at[along, core, zb, pl.ds(0, 11) if kind == 1 else pl.ds(11, 7)]

    def ring_copy(kind, d, t):
        ref = ring_piece(kind, d, t)
        dev = ((gx + (1 if d == 0 else 15)) % 16, gy, gz)
        return remote(ref, ref, zs.at[kind], zr.at[kind, d, t + 1], dev)

    def ring_wait(kind, d, t):
        bytes_of(ring_piece(kind, d, t), zr.at[kind, d, t]).wait()

    def piece(q, d, t):
        return G.at[q % 4, core, z_of(d, t)]

    def spread_copy(k, d, t):
        ref = piece(along, d, t)
        return remote(ref, ref, isn, ir.at[k - 1, d, t], weight_peer(k))

    def sibling_copy(q, d, t):
        ref = piece(q, d, t)
        return remote(ref, ref, sbs, sbr, (gx, gy, sib))

    def hand_out(d, t):
        for k in (2, 1, 3):
            spread_copy(k, d, t).start()
        sibling_copy(along, d, t).start()

    def take_in(d, t):
        for k in (1, 3, 2):
            bytes_of(piece(along + 4 - k, d, t), ir.at[k - 1, d, t]).wait()
            sibling_copy(along + 4 - k, d, t).start()

    def ring_step(t):
        for kind in range(3):
            for d in range(2):
                if t <= limit[d]:
                    ring_wait(kind, d, t)
                if t < limit[d]:
                    ring_copy(kind, d, t).start()
        for d in range(2):
            if t <= limit[d]:
                hand_out(d, t)

    def take_step(t):
        for d in range(2):
            if t <= limit[d] and (t > 0 or d == 0):
                take_in(d, t)

    def list_first(k):
        return remote(lists_in, LV.at[cx, cy], l1s.at[k - 1], l1r.at[k - 1], (gx, (gy + k) % 4, gz))

    def list_second(k):
        ref = LV.at[:, cy]
        return remote(ref, ref, l2s.at[k - 1], l2r.at[k - 1], (gx, gy, (gz + 2 * k) % 8))

    def first_copy(k):
        return remote(A.at[k - 1], B.at[:, :, first], a1s.at[k - 1], a1r.at[k - 1], tile_peer((first + k) % 4, second, core))

    def pick(k):
        f = (first + k) % 4

        def one(s, _):
            x = f + core * (s - f)
            y = s + core * (f - s)
            for n in range(8):
                tile = R[LS[x, y, gx, n]]
                if k == 0:
                    B[s, n, first] = tile
                else:
                    A[k - 1, s, n] = tile
            return 0

        lax.fori_loop(0, 4, one, 0)

    def second_copy(k, flip, m):
        c = core + flip * (1 - 2 * core)
        s, f = (second + k) % 4, (first + 4 - m) % 4
        return remote(
            B.at[s, pl.ds(c * 4, 4), f], F.at[core, :, f, second], a2s.at[k, flip, m], a2r.at[k, flip, m],
            tile_peer(first, s, c),
        )

    def second_send(m):
        for k, flip in second_all:
            second_copy(k, flip, m).start()

    second_all = ((2, 0), (2, 1), (1, 0), (1, 1), (3, 0), (3, 1), (0, 1))

    for kind in range(3):
        for d in range(2):
            ring_copy(kind, d, 0).start()
    for k in (1, 2, 3):
        list_first(k).start()
    halo_send(0)
    hand_out(0, 0)

    ring_step(1)
    ring_step(2)
    take_step(0)
    for k in (1, 2, 3):
        bytes_of(LV.at[(cx + 4 - k) % 4, cy], l1r.at[k - 1]).wait()
        list_first(k).wait_send()
    for k in (1, 2, 3):
        list_second(k).start()
    ring_step(3)
    take_step(1)
    own_s.wait()
    halo_middle(0)
    ring_step(4)
    take_step(2)
    column = lax.broadcasted_iota(jnp.int32, (768, 768), 1)
    natural = ((column & 255) >> 4) * 48 + (column >> 8) * 16 + (column & 15)
    order = (lax.broadcasted_iota(jnp.int32, (768, 768), 0) == natural).astype(BF)
    HP[...] = dot(head[...], order).astype(BF)
    ring_step(5)
    take_step(3)
    for k in (1, 2, 3):
        bytes_of(LV.at[:, (cy + 4 - k) % 4], l2r.at[k - 1]).wait()
        list_second(k).wait_send()
    to_smem = pltpu.make_async_copy(LV, LS, loc.at[3])
    to_smem.start()
    halo_end(0)
    ring_step(6)
    take_step(4)
    own_i.wait()
    own_h.wait()

    def reorder(s, _):
        IP[s] = dot(halves[...], IR[s]).astype(BF)
        return 0

    lax.fori_loop(0, 4, reorder, 0)
    ring_step(7)
    take_step(5)
    to_smem.wait()

    ring_wait(0, 0, 8)
    for k in (2, 1, 3):
        pick(k)
        first_copy(k).start()
    for kind in (1, 2):
        ring_wait(kind, 0, 8)
    hand_out(0, 8)
    pick(0)
    second_send(0)
    take_step(6)
    for k in (1, 3):
        bytes_of(B.at[:, :, (first + 4 - k) % 4], a1r.at[k - 1]).wait()
        second_send(k)
    take_step(7)
    bytes_of(B.at[:, :, (first + 2) % 4], a1r.at[1]).wait()
    second_send(2)
    take_step(8)
    stay = pltpu.make_async_copy(B.at[second, pl.ds(core * 4, 4)], F.at[core, :, :, second], loc.at[4])
    stay.start()
    bytes_of(G.at[:, 1 - core], sbr).wait()

    convolve_middle(block, False)
    convolve_sides(block, False)
    pre = ACC[...]
    hidden = (pre * jax.nn.sigmoid(pre)).astype(BF)
    halo_stage(1, hidden)
    halo_send(1)

    stay.wait()
    for k, flip in second_all:
        for m in range(4):
            bytes_of(F.at[core, :, 0, 0], a2r.at[k, flip, m]).wait()

    def teach(s, _):
        left = F[0, s].reshape(256, 256)
        right = F[1, s].reshape(256, 256)
        units = []
        for a in range(3):
            raw = dot_nt(left, block(27 + 2 * a)) + dot_nt(right, block(28 + 2 * a))
            units.append((raw * jax.nn.sigmoid(raw)).astype(BF))
        values = []
        for a in range(3):
            part = dot_nt(units[0], block(33 + 3 * a))
            part += dot_nt(units[1], block(34 + 3 * a))
            part += dot_nt(units[2], block(35 + 3 * a))
            values.append(part)
        power = sum(jnp.sum(v * v, axis=1, keepdims=True) for v in values)
        scale = lax.rsqrt(power * (1.0 / 768.0) + 1e-6)
        for a in range(3):
            FE[s, :, a * 256 : (a + 1) * 256] = (values[a] * scale).astype(BF)
        return 0

    def target(h, into):
        rows = pl.ds(pl.multiple_of(h * 256, 256), 256)

        def one(n, _):
            cols = pl.ds(pl.multiple_of(n * 256, 256), 256)
            total = dot(IP[0, rows], FE[0, :, cols])
            for s in range(1, 4):
                total += dot(IP[s, rows], FE[s, :, cols])
            into[:, cols] = total
            return 0

        lax.fori_loop(0, 3, one, 0)

    lax.fori_loop(0, 1, teach, 0)
    halo_middle(1)
    lax.fori_loop(1, 3, teach, 0)
    halo_end(1)
    lax.fori_loop(3, 4, teach, 0)
    target(1 - core, TS)
    swap = remote(TS, TR, ts, tr, (gx, gy, sib))
    swap.start()
    target(core, PP)

    convolve_middle(block_second, False)
    convolve_sides(block_second, False)
    pre = ACC[...]
    PRE[...] = pre
    SO[...] = (FA[1, 0:256].astype(F32) + pre * jax.nn.sigmoid(pre)).astype(BF)
    swap.wait()

    def head_part(n, _):
        cols = pl.ds(pl.multiple_of(n * 256, 256), 256)
        PP[:, cols] = dot(SO[...], HP[:, cols]) - (PP[:, cols] + TR[:, cols])
        return 0

    lax.fori_loop(0, 3, head_part, 0)
    back = dot_nt(PP[...].astype(BF), HP[...])
    GS[...] = back
    pre = PRE[...]
    gate = jax.nn.sigmoid(pre)
    halo_stage(2, (back * (gate * (1.0 + pre * (1.0 - gate)))).astype(BF))
    halo_send(2)

    def predict(n, _):
        cols = pl.ds(pl.multiple_of(n * 256, 256), 256)
        pred_out[:, cols] = dot(SO[...], head[:, cols]).astype(BF)
        return 0

    lax.fori_loop(0, 3, predict, 0)
    halo_middle(2)
    convolve_middle(block_second, True)
    halo_end(2)
    convolve_sides(block_second, True)
    grad_out[...] = (GS[...] + ACC[...]).astype(BF)

    bytes_of(R.at[pl.ds(0, 60)], zs.at[0]).wait()
    bytes_of(G.at[along, core, pl.ds(0, 15), pl.ds(0, 11)], zs.at[1]).wait()
    bytes_of(G.at[along, core, pl.ds(0, 15), pl.ds(11, 7)], zs.at[2]).wait()
    bytes_of(G.at[pl.ds(0, 3), core], isn).wait()
    bytes_of(G.at[:, core], sbs).wait()
    for k in (1, 2, 3):
        first_copy(k).wait_send()
    for k, flip in second_all:
        for m in range(4):
            second_copy(k, flip, m).wait_send()


def local(voxels, conv_first, conv_second, head_weight, teacher_in, teacher_out, tile_feats, interpolation, tile_lists):
    first = conv_first.transpose(0, 2, 1)
    second = conv_second.transpose(0, 2, 1)
    t_in = teacher_in.T.reshape(3, 16, 2, 256).transpose(0, 2, 1, 3).reshape(6, 16, 256)
    unit = np.arange(768)
    order = np.zeros((768, 768), np.float32)
    order[(unit % 256) // 16 * 48 + unit // 256 * 16 + unit % 16, unit] = 1
    t_out = dot(teacher_out.T, jnp.asarray(order, BF)).astype(BF)
    t_out = t_out.reshape(3, 16, 3, 256).transpose(0, 2, 1, 3).reshape(9, 16, 256)
    early = jnp.concatenate([first, t_in, t_out, jnp.zeros((2, 16, 256), BF)], axis=0).reshape(4, 11, 16, 256)
    late = jnp.concatenate([second, jnp.zeros((1, 16, 256), BF)], axis=0).reshape(4, 7, 16, 256)
    blob = jnp.concatenate([early, late], axis=1)
    lists = jnp.pad(tile_lists.reshape(16, 8), ((0, 0), (0, 120)))
    V = pltpu.VMEM
    D = pltpu.SemaphoreType.DMA
    scratch = [
        V((9, 256, 512), BF), V((512, 512), BF),
        V((4, 2, 16, 18, 16, 128), BF),
        V((64, 16, 256), BF),
        V((3, 4, 8, 16, 256), BF),
        V((4, 8, 4, 16, 256), BF),
        V((2, 4, 4, 4, 16, 256), BF),
        V((4, 512, 256), BF),
        V((4, 512, 256), BF),
        V((4, 256, 768), BF),
        V((256, 768), F32),
        V((256, 768), F32),
        V((3, 512, 256), BF),
        V((3, 256, 256), BF),
        V((3, 128, 256), BF),
        V((3, 128, 256), BF),
        V((9, 10, 32, 256), BF),
        V((4, 4, 16, 128), jnp.int32),
        pltpu.SMEM((4, 4, 16, 128), jnp.int32),
        V((256, 768), BF),
        V((256, 256), F32),
        V((256, 256), F32),
        V((256, 256), F32),
        V((256, 256), BF),
        V((256, 768), F32),
        D((7,)),
        D((3, 2, 9)), D((3,)),
        D((3, 2, 9)), D,
        D, D,
        D((3,)), D((3,)), D((3,)), D((3,)),
        D((3,)), D((3,)), D((4, 2, 4)), D((4, 2, 4)),
        D((3, 8)), D((3, 8)), D((3, 2)), D((3, 2)),
        D, D,
    ]
    vm = pl.BlockSpec(memory_space=pltpu.VMEM)
    hbm = pl.BlockSpec(memory_space=pl.ANY)
    prediction, hidden_grad = pl.pallas_call(
        kernel,
        out_shape=(jax.ShapeDtypeStruct((256, 768), BF), jax.ShapeDtypeStruct((256, 256), BF)),
        in_specs=[hbm, hbm, vm, vm, vm, hbm, hbm, vm, vm, vm, hbm],
        out_specs=(vm, vm),
        scratch_shapes=scratch,
        compiler_params=pltpu.CompilerParams(
            collective_id=0, has_side_effects=True, vmem_limit_bytes=56 * 1024 * 1024
        ),
        cost_estimate=pl.CostEstimate(flops=6_000_000_000, bytes_accessed=10_000_000, transcendentals=1_000_000),
    )(
        blob, tile_feats, lists, voxels.reshape(256, 256), head_weight, interpolation.reshape(8, 512, 256), *tables()
    )
    return prediction.reshape(8, 8, 4, 768), hidden_grad.reshape(8, 8, 4, 256)


def solution(mesh):
    in_specs = (
        P("gx", "gy", "gz", None),
        P(None, None, "gx"),
        P(None, None, "gx"),
        P(),
        P(None, "gx"),
        P(None, "gx"),
        P("gx", None, None),
        P(),
        P(None, "gy", "gz", None),
    )
    out_specs = (P("gx", "gy", "gz", None), P("gx", "gy", "gz", None))
    return jax.shard_map(local, mesh=mesh, in_specs=in_specs, out_specs=out_specs, check_vma=False)
```
